128 devices in a mesh: row: 8 (over z, y_hi), col: 16 (over x, y_lo, core).
Axes of the slice: x: 4, y: 4 (y_hi: 2, y_lo: 2; y = y_hi * 2 + y_lo), z: 4, core: 2. Of those that a mesh axis runs over, the one named last changes fastest.
Arguments:
- activations: float32 [128, 21504], P('row', 'col'), may hold values from -48 to 48
- out_grads: float32 [128, 5376], P('col', 'row'), may hold values from -6 to 6
- act_basis: bfloat16 [21504, 21504], P('col', 'row'), may hold values from -1.4 to 1.4
- grad_basis: bfloat16 [5376, 5376], P('row', 'col'), may hold values from -0.078125 to 0.078125
- eigenvalues: float32 [5376, 21504], P('col', 'row'), may hold values from 0.005 to 200, as said below
- query_ids: int32 [128], replicated, may hold values from 0 to 7, never falling along the last dimension, each value on 1 to 32 neighbouring positions
Outputs:
- inverse_product: float32 [2688, 21504], P('row', 'col')
The draws below stay inside these ranges and needn't reach their ends.
Inputs may be any that keep to these rules, and one draw needn't show every extreme that they name: `query_ids`: the ids never fall along the tokens; each of the 8 queries has 1 to 32 tokens, and one has exactly 32. `eigenvalues`: Positive.
All inputs are finite; a program needn't handle non-finite values.
Results may differ from the reference program's by a relative error of at most 0.034.
Values may be sent and summed in bfloat16 or wider, within the bound.
No kernel may reach another device: no remote copies, remote signals or barrier semaphores. Data moves between devices by JAX's collectives and lax.ppermute only.
A program may use at most 128 MiB of HBM per device.

```python
import math
import jax
import jax.numpy as jnp
import numpy as np
from jax import lax

WIDTH = 5376
INNER = 21504
TOKENS = 128
NQ = 8
QLEN = 32
ROWS = 2688
N_COL = 16


def draw_activations(key, part):
    key = jax.random.fold_in(key, 11)
    level_key, sample_key = jax.random.split(key)
    token_run = jnp.arange(TOKENS, dtype=jnp.int32) * 16 // TOKENS
    column_group = jnp.arange(INNER, dtype=jnp.int32) * 16 // INNER
    level_table = jnp.exp(jax.random.uniform(level_key, (16, 16), jnp.float32, -3.0, 3.0))
    levels = level_table[token_run][:, column_group]
    samples = jnp.clip(jax.random.normal(sample_key, (TOKENS, INNER), jnp.float32), -4.0, 4.0)
    return jnp.clip(samples * levels, -48.0, 48.0)


def draw_act_basis(key, part):
    key = jax.random.fold_in(key, 13)
    magnitude_key, sign_key, off_key = jax.random.split(key, 3)
    index = jnp.arange(INNER, dtype=jnp.int32)
    magnitude = jax.random.uniform(magnitude_key, (INNER,), jnp.float32, 0.6, 1.4)
    signs = jnp.where(jax.random.bernoulli(sign_key, 0.5, (INNER,)), 1.0, -1.0).astype(jnp.float32)
    scale = 1.0 / jnp.sqrt(jnp.float32(INNER))
    off_diag = jnp.clip(jax.random.normal(off_key, (INNER, INNER), jnp.float32), -6.0, 6.0) * scale
    on_diag = index[:, None] == index[None, :]
    return jnp.where(on_diag, (magnitude * signs)[None, :], off_diag).astype(jnp.bfloat16)


def draw_eigenvalues(key, part):
    key = jax.random.fold_in(key, 7)
    level_key, spread_key = jax.random.split(key)
    rows_pos = jnp.arange(WIDTH, dtype=jnp.float32)[:, None] / WIDTH
    cols_pos = jnp.arange(INNER, dtype=jnp.float32)[None, :] / INNER
    region_row = jnp.arange(WIDTH, dtype=jnp.int32) * 16 // WIDTH
    region_col = jnp.arange(INNER, dtype=jnp.int32) * 8 // INNER
    region_table = jnp.exp(jax.random.uniform(level_key, (16, 8), jnp.float32, -2.5, 2.5))
    region_level = region_table[region_row][:, region_col]
    spread = jnp.exp(jax.random.uniform(spread_key, (WIDTH, INNER), jnp.float32, -0.69, 0.69))
    base = 10.0 ** (0.5 - rows_pos) * 10.0 ** (0.5 - cols_pos) * spread
    return jnp.clip(base * region_level, 0.005, 200.0)


def block_scale(rng, dims, pieces, low, top_value):
    def one(position, blocks):
        draws = jax.random.uniform(jax.random.fold_in(jax.random.fold_in(rng, 6), position), (blocks,), jnp.float32, low / len(pieces), top_value / len(pieces))
        return jnp.repeat(jnp.exp(draws), dims[position] // blocks).reshape((-1,) + (1,) * (len(dims) - position - 1))

    loudness = one(*pieces[0])
    for cut in pieces[1:]:
        loudness = loudness * one(*cut)
    return loudness


def split_up(number_of, total, bound, slope):
    portions = [(1 << 20) // math.isqrt(grade ** slope) + 1 for grade in range(2, number_of + 1)]
    surplus, holding = total - bound - (number_of - 1), [1] * (number_of - 1)
    while surplus > 0:
        candidates = [i for i in range(number_of - 1) if holding[i] < bound]
        mass, remaining = sum([portions[i] for i in candidates]), surplus
        for i in candidates:
            addition = min(bound - holding[i], max(1, remaining * portions[i] // mass), surplus)
            holding[i] = holding[i] + addition
            surplus = surplus - addition
    return np.array([bound] + holding)


def ragged_sizes(own_key, count, total, reach, slope):
    if count == 2:
        one = jax.random.randint(own_key, (), max(1, total - reach), min(reach, total - 1) + 1)
        return jnp.stack([one, total - one])
    lengths = jnp.asarray(split_up(count, total, reach, slope), jnp.int32)
    couples = (count - 1) // 2
    giver, sink = lengths[1:1 + 2 * couples:2], lengths[2:2 + 2 * couples:2]
    slack = jnp.minimum(giver - 1, reach - sink)
    moved = jax.random.randint(jax.random.fold_in(own_key, 1), (couples,), 0, 1 << 20) % (slack + 1)
    lengths = lengths.at[1:1 + 2 * couples:2].set(giver - moved).at[2:2 + 2 * couples:2].set(sink + moved)
    return lengths[jax.random.permutation(jax.random.fold_in(own_key, 2), count)]


def normal_values(stream_key, shape, scale, most, shards=(), kind=jnp.bfloat16):
    entries = jax.random.normal(stream_key, shape, jnp.float32) * scale
    if len(shards) > 0:
        entries = block_scale(stream_key, shape, shards, -0.22, 0.18) * entries
    return jnp.clip(entries, min=-most, max=most).astype(kind)


def setup_inputs(seed: int = 0) -> dict:
    keys = jax.random.split(jax.random.key(seed), 7)
    return {
        "activations": draw_activations(jax.random.fold_in(keys[6], 71), 0),
        "out_grads": normal_values(keys[1], (TOKENS, WIDTH), 1.0, 6.0, ((0, 16), (1, 8)), jnp.float32),
        "act_basis": draw_act_basis(jax.random.fold_in(keys[6], 71), 0),
        "grad_basis": normal_values(keys[3], (WIDTH, WIDTH), WIDTH ** -0.5, 0.078125, ((0, 8), (1, 16))),
        "eigenvalues": draw_eigenvalues(jax.random.fold_in(keys[6], 71), 0),
        "query_ids": jnp.searchsorted(jnp.cumsum(ragged_sizes(keys[5], NQ, TOKENS, QLEN, 1)), jnp.arange(TOKENS), side="right").astype(jnp.int32),
    }


def reference(activations, out_grads, act_basis, grad_basis, eigenvalues, query_ids):
    act_bf = activations.astype(jnp.bfloat16)
    grad_bf = out_grads.astype(jnp.bfloat16)
    act_rot = jnp.dot(act_bf, act_basis, preferred_element_type=jnp.float32).astype(jnp.bfloat16)
    grad_rot = jnp.dot(grad_bf, grad_basis, preferred_element_type=jnp.float32).astype(jnp.bfloat16)
    damping = 0.1 * jnp.sum(eigenvalues) / (WIDTH * INNER)
    shifted = eigenvalues + damping

    def make_tile(query):
        picked = jnp.where((query_ids == query)[:, None], grad_rot, jnp.zeros_like(grad_rot))
        return jnp.dot(picked.T, act_rot, preferred_element_type=jnp.float32)

    def self_of(query):
        tile = make_tile(query)
        return jnp.sum(tile * tile / shifted) / (WIDTH * INNER)
    queries = jnp.arange(NQ, dtype=jnp.int32)
    self_infl = lax.map(self_of, queries)
    scales = 1.0 / jnp.sqrt(self_infl + 1e-06)

    def add_query(total, query):
        return (total + scales[query] * make_tile(query), None)
    total, unused = lax.scan(add_query, jnp.zeros((WIDTH, INNER), jnp.float32), queries)
    rotated = (total / shifted).astype(jnp.bfloat16)
    window = grad_basis[0::2]
    block = WIDTH // N_COL

    def add_block(index, summed):
        first = (index * block).astype(jnp.int32)
        w_part = lax.dynamic_slice_in_dim(window, first, block, 1)
        r_part = lax.dynamic_slice_in_dim(rotated, first, block, 0)
        partial_sum = jnp.dot(w_part, r_part, preferred_element_type=jnp.float32).astype(jnp.bfloat16)
        partial_sum = lax.optimization_barrier(partial_sum)
        return summed + partial_sum.astype(jnp.float32)
    left = lax.fori_loop(0, N_COL, add_block, jnp.zeros((ROWS, INNER), jnp.float32)).astype(jnp.bfloat16)
    return lax.dot_general(left, act_basis, (((1,), (1,)), ((), ())), preferred_element_type=jnp.float32)
```

```python
import functools

import jax
import jax.numpy as jnp
from jax import lax
from jax.experimental import pallas as pl
from jax.experimental.pallas import tpu as pltpu
from jax.sharding import Mesh, PartitionSpec as P

WIDTH = 5376
INNER = 21504
NQ = 8
TOKENS = 128
SIZES = {"z": 4, "h": 2, "x": 4, "l": 2, "k": 2}
ROW = ("z", "h")
COL = ("x", "l", "k")
ALL = ("z", "h", "x", "l", "k")
HALF = 168
SUB = 672
EBLK = 336
OUT = 1344
F32 = jnp.float32
BF16 = jnp.bfloat16


def shift(array, axis, by):
    size = SIZES[axis]
    return lax.ppermute(array, axis, [(i, (i + by) % size) for i in range(size)])


def gather(array, axes):
    count = 1
    for axis in axes:
        count *= SIZES[axis]
    spread = jnp.broadcast_to(array[None], (count,) + array.shape)
    return lax.all_to_all(spread, axes, 0, 0, tiled=True)


def left_kernel(order, w_ref, r_ref, mine_ref, other_ref):
    total = jnp.dot(w_ref[0, 0], r_ref[0], preferred_element_type=F32)
    for part in range(1, 4):
        total += jnp.dot(w_ref[0, part], r_ref[part], preferred_element_type=F32)
    mine_ref[0] = total[:HALF].astype(BF16)
    other_ref[0] = total[HALF:].astype(BF16)


def left_part(order, w_all, rotated):
    piece = jax.ShapeDtypeStruct((2, HALF, SUB), BF16)
    return pl.pallas_call(
        left_kernel,
        out_shape=(piece, piece),
        grid_spec=pltpu.PrefetchScalarGridSpec(
            num_scalar_prefetch=1,
            grid=(2,),
            in_specs=[
                pl.BlockSpec((1, 4, EBLK, EBLK), lambda h, order: (order[h], 0, 0, 0)),
                pl.BlockSpec((4, EBLK, SUB), lambda h, order: (0, 0, 0)),
            ],
            out_specs=[
                pl.BlockSpec((1, HALF, SUB), lambda h, order: (h, 0, 0)),
                pl.BlockSpec((1, HALF, SUB), lambda h, order: (h, 0, 0)),
            ],
        ),
        compiler_params=pltpu.CompilerParams(vmem_limit_bytes=32 * 1024 * 1024),
        cost_estimate=pl.CostEstimate(
            flops=2 * 672 * 1344 * 672, bytes_accessed=5 * 1024 * 1024, transcendentals=0
        ),
    )(order, w_all, rotated)


def product_kernel(with_sum, order, *refs):
    pieces = refs[:4]
    own_ref, far_ref = refs[4:6]
    sums = refs[6:8] if with_sum else None
    out0, out1, acc = refs[-3:]
    side = pl.program_id(0)
    part = pl.program_id(1)

    def step(left, basis):
        return lax.dot_general(left, basis, (((1,), (1,)), ((), ())), preferred_element_type=F32)

    for number in range(4):
        for which, basis in ((0, own_ref), (1, far_ref)):

            @pl.when((part == number) & (side == which))
            def _():
                term = step(pieces[number][...], basis[0])
                if number == 0:
                    acc[...] = term
                elif number < 3:
                    acc[...] += term
                else:
                    total = acc[...] + term
                    low, high = total[:HALF], total[HALF:]
                    if with_sum:
                        low += sums[0][0].astype(F32)
                        high += sums[1][0].astype(F32)
                    out0[0] = low.astype(BF16)
                    out1[0] = high.astype(BF16)


def product(order, pieces, own, far, sums):
    result = jax.ShapeDtypeStruct((2, HALF, OUT), BF16)
    whole = pl.BlockSpec((2 * HALF, SUB), lambda s, d, order: (0, 0))
    half = pl.BlockSpec((1, HALF, OUT), lambda s, d, order: (s, 0, 0))
    args = [*pieces, own, far]
    specs = [whole] * 4 + [
        pl.BlockSpec((1, OUT, SUB), lambda s, d, order: (order[jnp.where(s == 0, d, 3)], 0, 0)),
        pl.BlockSpec((1, OUT, SUB), lambda s, d, order: (order[jnp.where(s == 1, d, 0)], 0, 0)),
    ]
    if sums is not None:
        args += list(sums)
        specs += [half, half]
    return pl.pallas_call(
        functools.partial(product_kernel, sums is not None),
        out_shape=(result, result),
        grid_spec=pltpu.PrefetchScalarGridSpec(
            num_scalar_prefetch=1,
            grid=(2, 4),
            in_specs=specs,
            out_specs=[half, half],
            scratch_shapes=[pltpu.VMEM((2 * HALF, OUT), F32)],
        ),
        compiler_params=pltpu.CompilerParams(vmem_limit_bytes=40 * 1024 * 1024),
        cost_estimate=pl.CostEstimate(
            flops=2 * 336 * 2688 * 2688, bytes_accessed=22 * 1024 * 1024, transcendentals=0
        ),
    )(order, *args)


def shards(activations, out_grads, act_basis, grad_basis, eigenvalues, query_ids):
    z, h, x, k = (lax.axis_index(a) for a in ("z", "h", "x", "k"))

    act_all = gather(activations.astype(BF16), ROW).reshape(TOKENS, OUT)
    act_part = jnp.dot(act_all, act_basis, preferred_element_type=F32)
    act_part = (act_part + shift(act_part.astype(BF16), "k", 1).astype(F32)).astype(BF16)
    act_part = act_part.reshape(TOKENS, 4, SUB).transpose(1, 0, 2)
    act_part = jnp.sum(lax.all_to_all(act_part, "x", 0, 0, tiled=True).astype(F32), axis=0)
    act_rot = (act_part + shift(act_part.astype(BF16), "l", 1).astype(F32)).astype(BF16)

    grad_all = gather(out_grads.astype(BF16), COL).reshape(TOKENS, 672)
    grad_part = jnp.dot(grad_all, grad_basis, preferred_element_type=F32).astype(BF16)
    grad_own = jnp.sum(gather(grad_part, ROW).astype(F32), axis=0).astype(BF16)
    grad_rot = gather(grad_own, ("x",))

    window = grad_basis[0::2]
    window = jnp.where(k == 0, window, jnp.concatenate([window[HALF:], window[:HALF]], axis=0))
    w_all = lax.all_gather(window, ("z", "h", "x"), axis=0).reshape(8, 4, EBLK, EBLK)

    eig_part = eigenvalues.reshape(EBLK, 4, SUB).transpose(1, 0, 2).astype(BF16)
    eig = lax.all_to_all(eig_part, "x", 0, 0, tiled=True).astype(F32)
    basis_own = act_basis.reshape(OUT, 4, SUB).transpose(1, 0, 2)
    basis_far = shift(basis_own, "k", 1)

    eigen_total = jnp.sum(gather(jnp.full((1, 128), jnp.sum(eigenvalues)), ALL)[:, 0, 0])
    damping = 0.1 * eigen_total / (WIDTH * INNER)
    shifted = eig + damping

    queries = jnp.arange(NQ, dtype=jnp.int32)
    owned = query_ids[None, :] == queries[:, None]
    masked = jnp.where(owned[:, None, :, None], grad_rot[None], jnp.zeros_like(grad_rot)[None])
    tiles = jnp.einsum("qxtc,tf->qxcf", masked, act_rot, preferred_element_type=F32)
    local_self = jnp.sum(tiles * tiles / shifted[None], axis=(1, 2, 3))
    spread = jnp.broadcast_to(local_self[:, None], (NQ, 128))
    self_infl = jnp.sum(gather(spread, ALL), axis=0)[:, 0] / (WIDTH * INNER)
    scales = 1.0 / jnp.sqrt(self_infl + 1e-06)
    token_scale = jnp.sum(jnp.where(owned, scales[:, None], 0.0), axis=0)
    scaled = grad_rot.astype(F32) * token_scale[None, :, None]
    scaled_high = scaled.astype(BF16)
    scaled_low = (scaled - scaled_high.astype(F32)).astype(BF16)
    both = jnp.concatenate([scaled_high, scaled_low], axis=1)
    act_both = jnp.concatenate([act_rot, act_rot], axis=0)
    total = jnp.einsum("xtc,tf->xcf", both, act_both, preferred_element_type=F32)
    rotated = (total / shifted).astype(BF16)

    basis_order = (x - jnp.arange(4, dtype=jnp.int32)) % 4
    down = up = None
    sums = None
    for j in range(4):
        rows = jnp.stack([(z + 3 - j) % 4 * 2, (z + 1 + j) % 4 * 2 + 1]).astype(jnp.int32)
        mine, other = left_part(rows, w_all, rotated)
        pair = mine.astype(F32) + shift(other, "k", 1).astype(F32)
        sent = pair.astype(BF16)
        left = (sent.astype(F32) + shift(sent, "l", 1).astype(F32)).astype(BF16)
        left = left.reshape(2 * HALF, SUB)
        pieces = [left] + [shift(left, "x", d) for d in (1, 2, 3)]
        up, down = product(basis_order, pieces, basis_own, basis_far, sums)
        if j < 3:
            sums = (shift(up, "z", 1), shift(down, "z", 3))
    keep = jnp.where(h == 0, up, down)
    give = jnp.where(h == 0, down, up)
    both = (keep.astype(F32) + shift(give, "h", 1).astype(F32)).astype(BF16)
    near, away = both[0], both[1]
    back = shift(away, "k", 1)
    low = jnp.where(k == 0, near, back)
    high = jnp.where(k == 0, back, near)
    return jnp.concatenate([low, high], axis=0).astype(F32)


def solution(mesh):
    fine = Mesh(mesh.devices.reshape(tuple(SIZES.values())), tuple(SIZES))
    return jax.shard_map(
        shards,
        mesh=fine,
        in_specs=(P(ROW, COL), P(COL, ROW), P(COL, ROW), P(ROW, COL), P(COL, ROW), P()),
        out_specs=P(ROW, COL),
        check_vma=False,
    )
```

```python
import jax
import jax.numpy as jnp
from jax import lax
from jax.experimental import pallas as pl
from jax.experimental.pallas import tpu as pltpu
from jax.sharding import Mesh, PartitionSpec as P

WIDTH = 5376
INNER = 21504
NQ = 8
TOKENS = 128
SIZES = {"z": 4, "h": 2, "x": 4, "l": 2, "k": 2}
ROW = ("z", "h")
COL = ("x", "l", "k")
ALL = ("z", "h", "x", "l", "k")
HALF = 168
FREQ = 2688
SUBOWN = 672
STEP, SUB = 640, 768
COLS = 768
EBLK = 336
OUT = 1344
F32 = jnp.float32
BF16 = jnp.bfloat16
MIB = 1024 * 1024


def shift(array, axis, by):
    size = SIZES[axis]
    return lax.ppermute(array, axis, [(i, (i + by) % size) for i in range(size)])


def around(array, axis):
    return [array] + [shift(array, axis, by) for by in (1, 2, 3)]


def gather(array, axes):
    count = 1
    for axis in axes:
        count *= SIZES[axis]
    spread = jnp.broadcast_to(array[None], (count,) + array.shape)
    return lax.all_to_all(spread, axes, 0, 0, tiled=True)


def after(array, *others):
    return lax.optimization_barrier((array, others))[0]


def cut_kernel(eig_ref, *refs):
    values = eig_ref[...]
    for part in range(4):
        refs[part][...] = values[:, part * STEP : part * STEP + SUB].astype(BF16)
    refs[4][0] = jnp.sum(values.reshape(14, 8, FREQ), axis=0)


def cut_eigenvalues(eigenvalues):
    return pl.pallas_call(
        cut_kernel,
        out_shape=[jax.ShapeDtypeStruct((EBLK, SUB), BF16)] * 4 + [jax.ShapeDtypeStruct((3, 8, FREQ), F32)],
        grid=(3,),
        in_specs=[pl.BlockSpec((112, FREQ), lambda i: (i, 0))],
        out_specs=[pl.BlockSpec((112, SUB), lambda i: (i, 0))] * 4
        + [pl.BlockSpec((1, 8, FREQ), lambda i: (i, 0, 0))],
        compiler_params=pltpu.CompilerParams(vmem_limit_bytes=48 * MIB),
        cost_estimate=pl.CostEstimate(flops=10**6, bytes_accessed=6 * MIB, transcendentals=0),
    )(eigenvalues)


def left_kernel(rows, order, w_ref, own_ref, pair_ref, out_ref):
    total = None
    for part in range(4):
        for side, rot_ref in enumerate((own_ref, pair_ref)):
            term = jnp.dot(w_ref[0, order[part], side], rot_ref[part], preferred_element_type=F32)
            total = term if total is None else total + term
    out_ref[0] = total.astype(BF16)


def left_part(rows, order, windows, own, pair):
    return pl.pallas_call(
        left_kernel,
        out_shape=jax.ShapeDtypeStruct((2, HALF, SUB), BF16),
        grid_spec=pltpu.PrefetchScalarGridSpec(
            num_scalar_prefetch=2,
            grid=(2,),
            in_specs=[pl.BlockSpec((1, 4, 2, HALF, EBLK), lambda i, rows, order: (rows[i], 0, 0, 0, 0))]
            + [pl.BlockSpec((4, EBLK, SUB), lambda i, rows, order: (0, 0, 0))] * 2,
            out_specs=pl.BlockSpec((1, HALF, SUB), lambda i, rows, order: (i, 0, 0)),
        ),
        compiler_params=pltpu.CompilerParams(vmem_limit_bytes=60 * MIB),
        cost_estimate=pl.CostEstimate(
            flops=2 * 672 * 1344 * 672, bytes_accessed=6 * MIB, transcendentals=0
        ),
    )(rows, order, windows, own, pair)


def product_kernel(order, *refs):
    pieces = refs[:4]
    own_ref, far_ref, up_ref, down_ref = refs[4:]

    def step(basis_ref):
        total = None
        for number in range(4):
            first = pl.multiple_of(order[number] * STEP, 128)
            term = lax.dot_general(
                pieces[number][...],
                basis_ref[:, pl.ds(first, SUB)],
                (((1,), (1,)), ((), ())),
                preferred_element_type=F32,
            )
            total = term if total is None else total + term
        up_ref[0] = total[:HALF].astype(BF16)
        down_ref[0] = total[HALF:].astype(BF16)

    @pl.when(pl.program_id(0) == 0)
    def _():
        step(far_ref)

    @pl.when(pl.program_id(0) == 1)
    def _():
        step(own_ref)


def product(order, pieces, own, far):
    result = jax.ShapeDtypeStruct((2, HALF, OUT), BF16)
    half = pl.BlockSpec((1, HALF, COLS), lambda s, n, order: (s, 0, n))
    steps = pl.cdiv(OUT, COLS)
    return pl.pallas_call(
        product_kernel,
        out_shape=(result, result),
        grid_spec=pltpu.PrefetchScalarGridSpec(
            num_scalar_prefetch=1,
            grid=(2, steps),
            in_specs=[pl.BlockSpec((2 * HALF, SUB), lambda s, n, order: (0, 0))] * 4
            + [
                pl.BlockSpec((COLS, FREQ), lambda s, n, order: (jnp.where(s == 1, n, 0), 0)),
                pl.BlockSpec((COLS, FREQ), lambda s, n, order: (jnp.where(s == 0, n, steps - 1), 0)),
            ],
            out_specs=[half, half],
        ),
        compiler_params=pltpu.CompilerParams(vmem_limit_bytes=60 * MIB),
        cost_estimate=pl.CostEstimate(
            flops=2 * 336 * 2688 * 2688, bytes_accessed=18 * MIB, transcendentals=0
        ),
    )(order, *pieces, own, far)


def shards(activations, out_grads, act_basis, grad_basis, eigenvalues, query_ids):
    z, h, x, k = (lax.axis_index(a) for a in ("z", "h", "x", "k"))

    window = grad_basis[0::2]
    window = jnp.where(k == 0, window, jnp.concatenate([window[HALF:], window[:HALF]], axis=0))
    window = jnp.stack([window[:HALF], shift(window[HALF:], "k", 1)])
    windows = lax.all_gather(window, ("z", "h", "x"), axis=0).reshape(8, 4, 2, HALF, EBLK)

    grad_all = gather(after(out_grads.astype(BF16), window), COL).reshape(TOKENS, 672)
    grad_part = jnp.dot(grad_all, grad_basis, preferred_element_type=F32)
    grad_part = (grad_part + shift(grad_part.astype(BF16), "h", 1).astype(F32)).astype(BF16)
    grad_own = sum(piece.astype(F32) for piece in around(grad_part, "z")).astype(BF16)
    grad_rot = jnp.stack(around(grad_own, "x"))

    *eig_parts, eig_sums = cut_eigenvalues(eigenvalues)
    eig = [lax.select_n(x, *eig_parts)]
    eig += [shift(lax.select_n((x + by) % 4, *eig_parts), "x", by) for by in (1, 2, 3)]

    act_in = after(activations.astype(BF16), grad_all)
    act_all = gather(act_in, ROW).reshape(TOKENS, OUT)
    act_part = jnp.dot(act_all, act_basis, preferred_element_type=F32)
    eigen_in = after(jnp.full((1, 128), jnp.sum(eig_sums)), act_all)
    act_part = (act_part + shift(act_part.astype(BF16), "k", 1).astype(F32)).astype(BF16)
    act_part, eig = lax.optimization_barrier((act_part, eig))
    act_cuts = [act_part[:, c * STEP : c * STEP + SUB] for c in range(4)]
    act_sum = lax.select_n(x, *act_cuts).astype(F32)
    for by in (1, 2, 3):
        act_sum += shift(lax.select_n((x + by) % 4, *act_cuts), "x", by).astype(F32)
    place = lax.broadcasted_iota(jnp.int32, (1, SUB), 1) - (SUBOWN - STEP) * x
    act_sum = jnp.where((place >= 0) & (place < SUBOWN), act_sum, 0.0)
    act_rot = (act_sum + shift(act_sum.astype(BF16), "l", 1).astype(F32)).astype(BF16)
    basis_far = shift(act_basis, "k", 1)

    eigen_total = jnp.sum(gather(eigen_in, ALL)[:, 0, 0])
    damping = 0.1 * eigen_total / (WIDTH * INNER)
    shifted = jnp.stack(eig).astype(F32) + damping

    queries = jnp.arange(NQ, dtype=jnp.int32)
    owned = query_ids[None, :] == queries[:, None]
    masked = jnp.where(owned[:, None, :, None], grad_rot[None], jnp.zeros_like(grad_rot)[None])
    tiles = jnp.einsum("qxtc,tf->qxcf", masked, act_rot, preferred_element_type=F32)
    local_self = jnp.sum(tiles * tiles / shifted[None], axis=(1, 2, 3))
    spread = jnp.zeros((1, 128), F32).at[0, :NQ].set(local_self)
    self_infl = jnp.sum(gather(spread, ALL), axis=0)[0, :NQ] / (WIDTH * INNER)
    scales = 1.0 / jnp.sqrt(self_infl + 1e-06)
    token_scale = jnp.sum(jnp.where(owned, scales[:, None], 0.0), axis=0)
    scaled = grad_rot.astype(F32) * token_scale[None, :, None]
    scaled_high = scaled.astype(BF16)
    scaled_low = (scaled - scaled_high.astype(F32)).astype(BF16)
    both = jnp.concatenate([scaled_high, scaled_low], axis=1)
    act_both = jnp.concatenate([act_rot, act_rot], axis=0)
    total = jnp.einsum("xtc,tf->xcf", both, act_both, preferred_element_type=F32)
    rotated = (total / shifted).astype(BF16)
    rotated, basis_far = lax.optimization_barrier((rotated, basis_far))
    rotated_pair = shift(rotated, "k", 1)

    order = (x - jnp.arange(4, dtype=jnp.int32)) % 4
    ring = None
    for j in range(4):
        rows = jnp.stack([(z + 3 - j) % 4 * 2 + h, (z + 1 + j) % 4 * 2 + 1 - h]).astype(jnp.int32)
        sent = left_part(rows, order, windows, rotated, rotated_pair)
        left = (sent.astype(F32) + shift(sent, "l", 1).astype(F32)).astype(BF16)
        pieces = around(left.reshape(2 * HALF, SUB), "x")
        up, down = product(order, pieces, act_basis, basis_far)
        if ring is not None:
            up = (up.astype(F32) + ring[0].astype(F32)).astype(BF16)
            down = (down.astype(F32) + ring[1].astype(F32)).astype(BF16)
        if j < 3:
            ring = (shift(up, "z", 1), shift(down, "z", 3))
    done = (up.astype(F32) + shift(down, "h", 1).astype(F32)).astype(BF16)
    back = shift(done[0], "k", 1)
    low = jnp.where(k == 0, done[1], back)
    high = jnp.where(k == 0, back, done[1])
    return jnp.concatenate([low, high], axis=0).astype(F32)


def solution(mesh):
    fine = Mesh(mesh.devices.reshape(tuple(SIZES.values())), tuple(SIZES))
    return jax.shard_map(
        shards,
        mesh=fine,
        in_specs=(P(ROW, COL), P(COL, ROW), P(COL, ROW), P(ROW, COL), P(COL, ROW), P()),
        out_specs=P(ROW, COL),
        check_vma=False,
    )
```

```python
import jax
import jax.numpy as jnp
from jax import lax
from jax.experimental import pallas as pl
from jax.experimental.pallas import tpu as pltpu
from jax.sharding import Mesh, PartitionSpec as P

WIDTH = 5376
INNER = 21504
NQ = 8
TOKENS = 128
SIZES = {"z": 4, "h": 2, "x": 4, "l": 2, "k": 2}
ROW = ("z", "h")
COL = ("x", "l", "k")
ALL = ("z", "h", "x", "l", "k")
HALF = 168
FREQ = 2688
SUBOWN = 672
STEP, SUB = 640, 768
COLS = 768
EBLK = 336
OUT = 1344
F32 = jnp.float32
BF16 = jnp.bfloat16
MIB = 1024 * 1024


def shift(array, axis, by):
    size = SIZES[axis]
    return lax.ppermute(array, axis, [(i, (i + by) % size) for i in range(size)])


def around(array, axis):
    return [array] + [shift(array, axis, by) for by in (1, 2, 3)]


def gather(array, axes):
    count = 1
    for axis in axes:
        count *= SIZES[axis]
    spread = jnp.broadcast_to(array[None], (count,) + array.shape)
    return lax.all_to_all(spread, axes, 0, 0, tiled=True)


def after(array, *others):
    return lax.optimization_barrier((array, others))[0]


def cut_kernel(eig_ref, *refs):
    values = eig_ref[...]
    for part in range(4):
        refs[part][...] = values[:, part * STEP : part * STEP + SUB].astype(BF16)
    refs[4][0] = jnp.sum(values.reshape(14, 8, FREQ), axis=0)


def cut_eigenvalues(eigenvalues):
    return pl.pallas_call(
        cut_kernel,
        out_shape=[jax.ShapeDtypeStruct((EBLK, SUB), BF16)] * 4 + [jax.ShapeDtypeStruct((3, 8, FREQ), F32)],
        grid=(3,),
        in_specs=[pl.BlockSpec((112, FREQ), lambda i: (i, 0))],
        out_specs=[pl.BlockSpec((112, SUB), lambda i: (i, 0))] * 4
        + [pl.BlockSpec((1, 8, FREQ), lambda i: (i, 0, 0))],
        compiler_params=pltpu.CompilerParams(vmem_limit_bytes=48 * MIB),
        cost_estimate=pl.CostEstimate(flops=10**6, bytes_accessed=6 * MIB, transcendentals=0),
    )(eigenvalues)


def left_kernel(rows, order, w_ref, own_ref, pair_ref, out_ref):
    total = None
    for part in range(4):
        for side, rot_ref in enumerate((own_ref, pair_ref)):
            term = jnp.dot(w_ref[0, order[part], side], rot_ref[part], preferred_element_type=F32)
            total = term if total is None else total + term
    out_ref[0] = total.astype(BF16)


def left_part(rows, order, windows, own, pair):
    return pl.pallas_call(
        left_kernel,
        out_shape=jax.ShapeDtypeStruct((2, HALF, SUB), BF16),
        grid_spec=pltpu.PrefetchScalarGridSpec(
            num_scalar_prefetch=2,
            grid=(2,),
            in_specs=[pl.BlockSpec((1, 4, 2, HALF, EBLK), lambda i, rows, order: (rows[i], 0, 0, 0, 0))]
            + [pl.BlockSpec((4, EBLK, SUB), lambda i, rows, order: (0, 0, 0))] * 2,
            out_specs=pl.BlockSpec((1, HALF, SUB), lambda i, rows, order: (i, 0, 0)),
        ),
        compiler_params=pltpu.CompilerParams(vmem_limit_bytes=60 * MIB),
        cost_estimate=pl.CostEstimate(
            flops=2 * 672 * 1344 * 672, bytes_accessed=6 * MIB, transcendentals=0
        ),
    )(rows, order, windows, own, pair)


def three(value):
    high = value.astype(BF16)
    rest = value - high.astype(F32)
    middle = rest.astype(BF16)
    return jnp.stack([high, middle, (rest - middle.astype(F32)).astype(BF16)])


def product_kernel(order, *refs):
    pieces = refs[:4]
    own_ref, far_ref, up_ref, down_ref = refs[4:]

    def step(basis_ref):
        total = None
        for number in range(4):
            first = pl.multiple_of(order[number] * STEP, 128)
            term = lax.dot_general(
                pieces[number][...],
                basis_ref[:, pl.ds(first, SUB)],
                (((1,), (1,)), ((), ())),
                preferred_element_type=F32,
            )
            total = term if total is None else total + term
        up_ref[0] = total[:HALF].astype(BF16)
        down_ref[0] = total[HALF:].astype(BF16)

    @pl.when(pl.program_id(0) == 0)
    def _():
        step(far_ref)

    @pl.when(pl.program_id(0) == 1)
    def _():
        step(own_ref)


def product(order, pieces, own, far):
    result = jax.ShapeDtypeStruct((2, HALF, OUT), BF16)
    half = pl.BlockSpec((1, HALF, COLS), lambda s, n, order: (s, 0, n))
    steps = pl.cdiv(OUT, COLS)
    return pl.pallas_call(
        product_kernel,
        out_shape=(result, result),
        grid_spec=pltpu.PrefetchScalarGridSpec(
            num_scalar_prefetch=1,
            grid=(2, steps),
            in_specs=[pl.BlockSpec((2 * HALF, SUB), lambda s, n, order: (0, 0))] * 4
            + [
                pl.BlockSpec((COLS, FREQ), lambda s, n, order: (jnp.where(s == 1, n, 0), 0)),
                pl.BlockSpec((COLS, FREQ), lambda s, n, order: (jnp.where(s == 0, n, steps - 1), 0)),
            ],
            out_specs=[half, half],
        ),
        compiler_params=pltpu.CompilerParams(vmem_limit_bytes=60 * MIB),
        cost_estimate=pl.CostEstimate(
            flops=2 * 336 * 2688 * 2688, bytes_accessed=18 * MIB, transcendentals=0
        ),
    )(order, *pieces, own, far)


def shards(activations, out_grads, act_basis, grad_basis, eigenvalues, query_ids):
    z, h, x, k = (lax.axis_index(a) for a in ("z", "h", "x", "k"))

    window = grad_basis[0::2]
    window = jnp.where(k == 0, window, jnp.concatenate([window[HALF:], window[:HALF]], axis=0))
    window = jnp.stack([window[:HALF], shift(window[HALF:], "k", 1)])
    windows = lax.all_gather(window, ("z", "h", "x"), axis=0).reshape(8, 4, 2, HALF, EBLK)

    *eig_parts, eig_sums = cut_eigenvalues(eigenvalues)
    tail = jnp.zeros((8, 96), BF16).at[0, :3].set(three(jnp.sum(eig_sums)))
    grad_in = jnp.concatenate([out_grads.astype(BF16), tail], axis=1)
    grad_all = gather(grad_in, COL).reshape(TOKENS, 768)
    eig_col = jnp.sum(grad_all[0::8, 672:675].astype(F32))

    act_all = gather(after(activations.astype(BF16), grad_all), ROW).reshape(TOKENS, OUT)

    eig_parts = after(eig_parts, grad_all)
    eig = [lax.select_n(x, *eig_parts)]
    eig += [shift(lax.select_n((x + by) % 4, *eig_parts), "x", by) for by in (1, 2, 3)]

    grad_part = jnp.dot(grad_all[:, :672], grad_basis, preferred_element_type=F32)

    def with_sum(part, total):
        return jnp.concatenate([part.astype(BF16), jnp.zeros((TOKENS, 48), BF16).at[0, :3].set(three(total))], axis=1)

    pair = shift(with_sum(grad_part, eig_col), "h", 1).astype(F32)
    grad_part = grad_part + pair[:, :EBLK]
    pieces = around(with_sum(grad_part, eig_col + jnp.sum(pair[0, EBLK : EBLK + 3])), "z")
    summed = sum(piece.astype(F32) for piece in pieces)
    grad_own = summed[:, :EBLK].astype(BF16)
    damping = 0.1 * jnp.sum(summed[0, EBLK : EBLK + 3]) / (WIDTH * INNER)

    act_all, grad_own, eig = lax.optimization_barrier((act_all, grad_own, eig))
    act_part = jnp.dot(act_all, act_basis, preferred_element_type=F32)
    act_part = (act_part + shift(act_part.astype(BF16), "k", 1).astype(F32)).astype(BF16)
    act_cuts = [act_part[:, c * STEP : c * STEP + SUB] for c in range(4)]
    act_sum = lax.select_n(x, *act_cuts).astype(F32)
    for by in (1, 2, 3):
        act_sum += shift(lax.select_n((x + by) % 4, *act_cuts), "x", by).astype(F32)
    grad_rot = jnp.stack(around(after(grad_own, act_part), "x"))
    place = lax.broadcasted_iota(jnp.int32, (1, SUB), 1) - (SUBOWN - STEP) * x
    act_sum = jnp.where((place >= 0) & (place < SUBOWN), act_sum, 0.0)
    act_rot = (act_sum + shift(act_sum.astype(BF16), "l", 1).astype(F32)).astype(BF16)
    basis_far = shift(act_basis, "k", 1)

    shifted = jnp.stack(eig).astype(F32) + damping

    queries = jnp.arange(NQ, dtype=jnp.int32)
    owned = query_ids[None, :] == queries[:, None]
    masked = jnp.where(owned[:, None, :, None], grad_rot[None], jnp.zeros_like(grad_rot)[None])
    tiles = jnp.einsum("qxtc,tf->qxcf", masked, act_rot, preferred_element_type=F32)
    local_self = jnp.sum(tiles * tiles / shifted[None], axis=(1, 2, 3))
    spread = jnp.zeros((1, 128), F32).at[0, :NQ].set(local_self)
    self_infl = jnp.sum(gather(spread, ALL), axis=0)[0, :NQ] / (WIDTH * INNER)
    scales = 1.0 / jnp.sqrt(self_infl + 1e-06)
    token_scale = jnp.sum(jnp.where(owned, scales[:, None], 0.0), axis=0)
    scaled = grad_rot.astype(F32) * token_scale[None, :, None]
    scaled_high = scaled.astype(BF16)
    scaled_low = (scaled - scaled_high.astype(F32)).astype(BF16)
    both = jnp.concatenate([scaled_high, scaled_low], axis=1)
    act_both = jnp.concatenate([act_rot, act_rot], axis=0)
    total = jnp.einsum("xtc,tf->xcf", both, act_both, preferred_element_type=F32)
    rotated = (total / shifted).astype(BF16)
    rotated, basis_far = lax.optimization_barrier((rotated, basis_far))
    rotated_pair = shift(rotated, "k", 1)

    order = (x - jnp.arange(4, dtype=jnp.int32)) % 4
    lefts = []
    for j in range(4):
        rows = jnp.stack([(z + 3 - j) % 4 * 2 + h, (z + 1 + j) % 4 * 2 + 1 - h]).astype(jnp.int32)
        lefts.append(left_part(rows, order, windows, rotated, rotated_pair))
    ring = None
    sums = []
    for j in range(4):
        left = (lefts[j].astype(F32) + shift(lefts[j], "l", 1).astype(F32)).astype(BF16)
        pieces = around(left.reshape(2 * HALF, SUB), "x")
        pieces = after(pieces, *(sums[j - 1] if j > 0 else lefts))
        up, down = product(order, pieces, act_basis, basis_far)
        if j == 3:
            break
        if ring is not None:
            up = (up.astype(F32) + ring[0].astype(F32)).astype(BF16)
            down = (down.astype(F32) + ring[1].astype(F32)).astype(BF16)
        sums.append((up, down))
        if j < 2:
            ring = (shift(up, "z", 1), shift(down, "z", 3))

    def finish(side):
        arrived_up, arrived_down = lax.optimization_barrier(
            (shift(sums[2][0][side], "z", 1), shift(sums[2][1][side], "z", 3))
        )
        give = (down[side].astype(F32) + arrived_down.astype(F32)).astype(BF16)
        keep = up[side].astype(F32) + arrived_up.astype(F32)
        return (keep + shift(give, "h", 1).astype(F32)).astype(BF16)

    done = [finish(0), finish(1)]
    back = shift(done[0], "k", 1)
    low = jnp.where(k == 0, done[1], back)
    high = jnp.where(k == 0, back, done[1])
    return jnp.concatenate([low, high], axis=0).astype(F32)


def solution(mesh):
    fine = Mesh(mesh.devices.reshape(tuple(SIZES.values())), tuple(SIZES))
    return jax.shard_map(
        shards,
        mesh=fine,
        in_specs=(P(ROW, COL), P(COL, ROW), P(COL, ROW), P(ROW, COL), P(COL, ROW), P()),
        out_specs=P(ROW, COL),
        check_vma=False,
    )
```

```python
import jax
import jax.numpy as jnp
from jax import lax
from jax.experimental import pallas as pl
from jax.experimental.pallas import tpu as pltpu
from jax.sharding import Mesh, PartitionSpec as P

WIDTH = 5376
INNER = 21504
NQ = 8
TOKENS = 128
SIZES = {"z": 4, "h": 2, "x": 4, "l": 2, "k": 2}
ROW = ("z", "h")
COL = ("x", "l", "k")
ALL = ("z", "h", "x", "l", "k")
HALF = 168
FREQ = 2688
SUBOWN = 672
STEP, SUB = 640, 768
COLS = 768
EBLK = 336
OUT = 1344
F32 = jnp.float32
BF16 = jnp.bfloat16
MIB = 1024 * 1024


def shift(array, axis, by):
    size = SIZES[axis]
    return lax.ppermute(array, axis, [(i, (i + by) % size) for i in range(size)])


def around(array, axis):
    return [array] + [shift(array, axis, by) for by in (1, 2, 3)]


def gather(array, axes):
    count = 1
    for axis in axes:
        count *= SIZES[axis]
    spread = jnp.broadcast_to(array[None], (count,) + array.shape)
    return lax.all_to_all(spread, axes, 0, 0, tiled=True)


def after(array, *others):
    return lax.optimization_barrier((array, others))[0]


def cut_kernel(eig_ref, *refs):
    values = eig_ref[...]
    for part in range(4):
        refs[part][...] = values[:, part * STEP : part * STEP + SUB].astype(BF16)
    refs[4][0] = jnp.sum(values.reshape(14, 8, FREQ), axis=0)


def cut_eigenvalues(eigenvalues):
    return pl.pallas_call(
        cut_kernel,
        out_shape=[jax.ShapeDtypeStruct((EBLK, SUB), BF16)] * 4 + [jax.ShapeDtypeStruct((3, 8, FREQ), F32)],
        grid=(3,),
        in_specs=[pl.BlockSpec((112, FREQ), lambda i: (i, 0))],
        out_specs=[pl.BlockSpec((112, SUB), lambda i: (i, 0))] * 4
        + [pl.BlockSpec((1, 8, FREQ), lambda i: (i, 0, 0))],
        compiler_params=pltpu.CompilerParams(vmem_limit_bytes=48 * MIB),
        cost_estimate=pl.CostEstimate(flops=10**6, bytes_accessed=6 * MIB, transcendentals=0),
    )(eigenvalues)


def left_kernel(rows, order, w_ref, own_ref, pair_ref, out_ref):
    total = None
    for part in range(4):
        for side, rot_ref in enumerate((own_ref, pair_ref)):
            term = jnp.dot(w_ref[0, order[part], side], rot_ref[part], preferred_element_type=F32)
            total = term if total is None else total + term
    out_ref[0] = total.astype(BF16)


def left_part(rows, order, windows, own, pair):
    return pl.pallas_call(
        left_kernel,
        out_shape=jax.ShapeDtypeStruct((2, HALF, SUB), BF16),
        grid_spec=pltpu.PrefetchScalarGridSpec(
            num_scalar_prefetch=2,
            grid=(2,),
            in_specs=[pl.BlockSpec((1, 4, 2, HALF, EBLK), lambda i, rows, order: (rows[i], 0, 0, 0, 0))]
            + [pl.BlockSpec((4, EBLK, SUB), lambda i, rows, order: (0, 0, 0))] * 2,
            out_specs=pl.BlockSpec((1, HALF, SUB), lambda i, rows, order: (i, 0, 0)),
        ),
        compiler_params=pltpu.CompilerParams(vmem_limit_bytes=54 * MIB),
        cost_estimate=pl.CostEstimate(
            flops=2 * 672 * 1344 * 672, bytes_accessed=6 * MIB, transcendentals=0
        ),
    )(rows, order, windows, own, pair)


def three(value):
    high = value.astype(BF16)
    rest = value - high.astype(F32)
    middle = rest.astype(BF16)
    return jnp.stack([high, middle, (rest - middle.astype(F32)).astype(BF16)])


def product_kernel(order, *refs):
    pieces = refs[:4]
    own_ref, far_ref, up_ref, down_ref = refs[4:]

    def step(basis_ref):
        total = None
        for number in range(4):
            first = pl.multiple_of(order[number] * STEP, 128)
            term = lax.dot_general(
                pieces[number][...],
                basis_ref[:, pl.ds(first, SUB)],
                (((1,), (1,)), ((), ())),
                preferred_element_type=F32,
            )
            total = term if total is None else total + term
        up_ref[0] = total[:HALF].astype(BF16)
        down_ref[0] = total[HALF:].astype(BF16)

    @pl.when(pl.program_id(0) == 0)
    def _():
        step(far_ref)

    @pl.when(pl.program_id(0) == 1)
    def _():
        step(own_ref)


def side_kernel(order, *refs):
    pieces = refs[:4]
    basis_ref, up_ref, down_ref = refs[4:]
    total = None
    for number in range(4):
        first = pl.multiple_of(order[number] * STEP, 128)
        term = lax.dot_general(
            pieces[number][...],
            basis_ref[:, pl.ds(first, SUB)],
            (((1,), (1,)), ((), ())),
            preferred_element_type=F32,
        )
        total = term if total is None else total + term
    up_ref[...] = total[:HALF].astype(BF16)
    down_ref[...] = total[HALF:].astype(BF16)


def side_product(order, pieces, basis):
    result = jax.ShapeDtypeStruct((HALF, OUT), BF16)
    half = pl.BlockSpec((HALF, COLS), lambda n, order: (0, n))
    return pl.pallas_call(
        side_kernel,
        out_shape=(result, result),
        grid_spec=pltpu.PrefetchScalarGridSpec(
            num_scalar_prefetch=1,
            grid=(pl.cdiv(OUT, COLS),),
            in_specs=[pl.BlockSpec((2 * HALF, SUB), lambda n, order: (0, 0))] * 4
            + [pl.BlockSpec((COLS, FREQ), lambda n, order: (n, 0))],
            out_specs=[half, half],
        ),
        compiler_params=pltpu.CompilerParams(vmem_limit_bytes=60 * MIB),
        cost_estimate=pl.CostEstimate(
            flops=336 * 2688 * 2688, bytes_accessed=10 * MIB, transcendentals=0
        ),
    )(order, *pieces, basis)


def product(order, pieces, own, far):
    result = jax.ShapeDtypeStruct((2, HALF, OUT), BF16)
    half = pl.BlockSpec((1, HALF, COLS), lambda s, n, order: (s, 0, n))
    steps = pl.cdiv(OUT, COLS)
    return pl.pallas_call(
        product_kernel,
        out_shape=(result, result),
        grid_spec=pltpu.PrefetchScalarGridSpec(
            num_scalar_prefetch=1,
            grid=(2, steps),
            in_specs=[pl.BlockSpec((2 * HALF, SUB), lambda s, n, order: (0, 0))] * 4
            + [
                pl.BlockSpec((COLS, FREQ), lambda s, n, order: (jnp.where(s == 1, n, 0), 0)),
                pl.BlockSpec((COLS, FREQ), lambda s, n, order: (jnp.where(s == 0, n, steps - 1), 0)),
            ],
            out_specs=[half, half],
        ),
        compiler_params=pltpu.CompilerParams(vmem_limit_bytes=60 * MIB),
        cost_estimate=pl.CostEstimate(
            flops=2 * 336 * 2688 * 2688, bytes_accessed=18 * MIB, transcendentals=0
        ),
    )(order, *pieces, own, far)


def shards(activations, out_grads, act_basis, grad_basis, eigenvalues, query_ids):
    z, h, x, k = (lax.axis_index(a) for a in ("z", "h", "x", "k"))

    window = grad_basis[0::2]
    window = jnp.where(k == 0, window, jnp.concatenate([window[HALF:], window[:HALF]], axis=0))
    window = jnp.stack([window[:HALF], shift(window[HALF:], "k", 1)])
    windows = lax.all_gather(window, ("z", "h", "x"), axis=0).reshape(8, 4, 2, HALF, EBLK)

    *eig_parts, eig_sums = cut_eigenvalues(eigenvalues)
    tail = jnp.zeros((8, 96), BF16).at[0, :3].set(three(jnp.sum(eig_sums)))
    grad_in = jnp.concatenate([out_grads.astype(BF16), tail], axis=1)
    grad_all = gather(grad_in, COL).reshape(TOKENS, 768)
    eig_col = jnp.sum(grad_all[0::8, 672:675].astype(F32))

    act_all = gather(after(activations.astype(BF16), grad_all), ROW).reshape(TOKENS, OUT)

    eig_parts = after(eig_parts, grad_all)
    eig = [lax.select_n(x, *eig_parts)]
    eig += [shift(lax.select_n((x + by) % 4, *eig_parts), "x", by) for by in (1, 2, 3)]

    grad_part = jnp.dot(grad_all[:, :672], grad_basis, preferred_element_type=F32)

    def with_sum(part, total):
        return jnp.concatenate([part.astype(BF16), jnp.zeros((TOKENS, 48), BF16).at[0, :3].set(three(total))], axis=1)

    pair = shift(with_sum(grad_part, eig_col), "h", 1).astype(F32)
    grad_part = grad_part + pair[:, :EBLK]
    pieces = around(with_sum(grad_part, eig_col + jnp.sum(pair[0, EBLK : EBLK + 3])), "z")
    summed = sum(piece.astype(F32) for piece in pieces)
    grad_own = summed[:, :EBLK].astype(BF16)
    damping = 0.1 * jnp.sum(summed[0, EBLK : EBLK + 3]) / (WIDTH * INNER)

    act_all, grad_own, eig = lax.optimization_barrier((act_all, grad_own, eig))
    act_part = jnp.dot(act_all, act_basis, preferred_element_type=F32)
    act_part = (act_part + shift(act_part.astype(BF16), "k", 1).astype(F32)).astype(BF16)
    act_cuts = [act_part[:, c * STEP : c * STEP + SUB] for c in range(4)]
    act_sum = lax.select_n(x, *act_cuts).astype(F32)
    for by in (1, 2, 3):
        act_sum += shift(lax.select_n((x + by) % 4, *act_cuts), "x", by).astype(F32)
    grad_rot = jnp.stack(around(after(grad_own, act_sum), "x"))
    place = lax.broadcasted_iota(jnp.int32, (1, SUB), 1) - (SUBOWN - STEP) * x
    act_sum = jnp.where((place >= 0) & (place < SUBOWN), act_sum, 0.0)
    act_rot = (act_sum + shift(act_sum.astype(BF16), "l", 1).astype(F32)).astype(BF16)
    basis_far = shift(act_basis, "k", 1)

    shifted = jnp.stack(eig).astype(F32) + damping

    queries = jnp.arange(NQ, dtype=jnp.int32)
    owned = query_ids[None, :] == queries[:, None]
    masked = jnp.where(owned[:, None, :, None], grad_rot[None], jnp.zeros_like(grad_rot)[None])
    tiles = jnp.einsum("qxtc,tf->qxcf", masked, act_rot, preferred_element_type=F32)
    local_self = jnp.sum(tiles * tiles / shifted[None], axis=(1, 2, 3))
    spread = jnp.zeros((1, 128), F32).at[0, :NQ].set(local_self)
    self_infl = jnp.sum(gather(spread, ALL), axis=0)[0, :NQ] / (WIDTH * INNER)
    scales = 1.0 / jnp.sqrt(self_infl + 1e-06)
    token_scale = jnp.sum(jnp.where(owned, scales[:, None], 0.0), axis=0)
    scaled = grad_rot.astype(F32) * token_scale[None, :, None]
    scaled_high = scaled.astype(BF16)
    scaled_low = (scaled - scaled_high.astype(F32)).astype(BF16)
    both = jnp.concatenate([scaled_high, scaled_low], axis=1)
    act_both = jnp.concatenate([act_rot, act_rot], axis=0)
    total = jnp.einsum("xtc,tf->xcf", both, act_both, preferred_element_type=F32)
    rotated = (total / shifted).astype(BF16)
    rotated, basis_far = lax.optimization_barrier((rotated, basis_far))
    rotated_pair = shift(rotated, "k", 1)

    order = (x - jnp.arange(4, dtype=jnp.int32)) % 4
    lefts = []
    for j in range(4):
        rows = jnp.stack([(z + 3 - j) % 4 * 2 + h, (z + 1 + j) % 4 * 2 + 1 - h]).astype(jnp.int32)
        lefts.append(left_part(rows, order, windows, rotated, rotated_pair))
    summed = [(part.astype(F32) + shift(part, "l", 1).astype(F32)).astype(BF16) for part in lefts]
    ring = None
    sums = []
    for j in range(4):
        pieces = around(summed[j].reshape(2 * HALF, SUB), "x")
        pieces = after(pieces, *(sums[j - 1] if j > 0 else lefts))
        if j == 3:
            break
        up, down = product(order, pieces, act_basis, basis_far)
        if ring is not None:
            up = (up.astype(F32) + ring[0].astype(F32)).astype(BF16)
            down = (down.astype(F32) + ring[1].astype(F32)).astype(BF16)
        sums.append((up, down))
        if j < 2:
            ring = (shift(up, "z", 1), shift(down, "z", 3))

    arrived = [
        lax.optimization_barrier((shift(sums[2][0][side], "z", 1), shift(sums[2][1][side], "z", 3)))
        for side in range(2)
    ]
    done = []
    give = ()
    for side, basis in enumerate((basis_far, act_basis)):
        up, down = side_product(order, after(pieces, *give), basis)
        give = ((down.astype(F32) + arrived[side][1].astype(F32)).astype(BF16),)
        keep = up.astype(F32) + arrived[side][0].astype(F32)
        done.append((keep + shift(give[0], "h", 1).astype(F32)).astype(BF16))
    back = shift(done[0], "k", 1)
    low = jnp.where(k == 0, done[1], back)
    high = jnp.where(k == 0, back, done[1])
    return jnp.concatenate([low, high], axis=0).astype(F32)


def solution(mesh):
    fine = Mesh(mesh.devices.reshape(tuple(SIZES.values())), tuple(SIZES))
    return jax.shard_map(
        shards,
        mesh=fine,
        in_specs=(P(ROW, COL), P(COL, ROW), P(COL, ROW), P(ROW, COL), P(COL, ROW), P()),
        out_specs=P(ROW, COL),
        check_vma=False,
    )
```

```python
import jax
import jax.numpy as jnp
from jax import lax
from jax.experimental import pallas as pl
from jax.experimental.pallas import tpu as pltpu
from jax.sharding import Mesh, PartitionSpec as P

WIDTH = 5376
INNER = 21504
NQ = 8
TOKENS = 128
SIZES = {"z": 4, "h": 2, "x": 4, "l": 2, "k": 2}
ROW = ("z", "h")
COL = ("x", "l", "k")
ALL = ("z", "h", "x", "l", "k")
HALF = 168
FREQ = 2688
SUBOWN = 672
STEP, SUB = 640, 768
COLS = 768
EBLK = 336
OUT = 1344
F32 = jnp.float32
BF16 = jnp.bfloat16
MIB = 1024 * 1024


def shift(array, axis, by):
    size = SIZES[axis]
    return lax.ppermute(array, axis, [(i, (i + by) % size) for i in range(size)])


def around(array, axis):
    return [array] + [shift(array, axis, by) for by in (1, 2, 3)]


def gather(array, axes):
    count = 1
    for axis in axes:
        count *= SIZES[axis]
    spread = jnp.broadcast_to(array[None], (count,) + array.shape)
    return lax.all_to_all(spread, axes, 0, 0, tiled=True)


def after(array, *others):
    return lax.optimization_barrier((array, others))[0]


def cut_kernel(eig_ref, *refs):
    values = eig_ref[...]
    for part in range(4):
        refs[part][...] = values[:, part * STEP : part * STEP + SUB].astype(BF16)
    refs[4][0] = jnp.sum(values.reshape(14, 8, FREQ), axis=0)


def cut_eigenvalues(eigenvalues):
    return pl.pallas_call(
        cut_kernel,
        out_shape=[jax.ShapeDtypeStruct((EBLK, SUB), BF16)] * 4 + [jax.ShapeDtypeStruct((3, 8, FREQ), F32)],
        grid=(3,),
        in_specs=[pl.BlockSpec((112, FREQ), lambda i: (i, 0))],
        out_specs=[pl.BlockSpec((112, SUB), lambda i: (i, 0))] * 4
        + [pl.BlockSpec((1, 8, FREQ), lambda i: (i, 0, 0))],
        compiler_params=pltpu.CompilerParams(vmem_limit_bytes=48 * MIB),
        cost_estimate=pl.CostEstimate(flops=10**6, bytes_accessed=6 * MIB, transcendentals=0),
    )(eigenvalues)


def left_kernel(rows, order, w_ref, own_ref, pair_ref, out_ref):
    total = None
    for part in range(4):
        for side, rot_ref in enumerate((own_ref, pair_ref)):
            term = jnp.dot(w_ref[0, order[part], 0, side], rot_ref[part], preferred_element_type=F32)
            total = term if total is None else total + term
    out_ref[0] = total.astype(BF16)


def left_part(rows, order, windows, own, pair):
    return pl.pallas_call(
        left_kernel,
        out_shape=jax.ShapeDtypeStruct((2, HALF, SUB), BF16),
        grid_spec=pltpu.PrefetchScalarGridSpec(
            num_scalar_prefetch=2,
            grid=(2,),
            in_specs=[pl.BlockSpec((1, 4, 1, 2, HALF, EBLK), lambda i, rows, order: (rows[i], 0, i, 0, 0, 0))]
            + [pl.BlockSpec((4, EBLK, SUB), lambda i, rows, order: (0, 0, 0))] * 2,
            out_specs=pl.BlockSpec((1, HALF, SUB), lambda i, rows, order: (i, 0, 0)),
        ),
        compiler_params=pltpu.CompilerParams(vmem_limit_bytes=54 * MIB),
        cost_estimate=pl.CostEstimate(
            flops=2 * 672 * 1344 * 672, bytes_accessed=6 * MIB, transcendentals=0
        ),
    )(rows, order, windows, own, pair)


def three(value):
    high = value.astype(BF16)
    rest = value - high.astype(F32)
    middle = rest.astype(BF16)
    return jnp.stack([high, middle, (rest - middle.astype(F32)).astype(BF16)])


def product_kernel(order, *refs):
    pieces = refs[:4]
    own_ref, far_ref, up_ref, down_ref = refs[4:]

    def step(basis_ref):
        total = None
        for number in range(4):
            first = pl.multiple_of(order[number] * STEP, 128)
            term = lax.dot_general(
                pieces[number][...],
                basis_ref[:, pl.ds(first, SUB)],
                (((1,), (1,)), ((), ())),
                preferred_element_type=F32,
            )
            total = term if total is None else total + term
        up_ref[0] = total[:HALF].astype(BF16)
        down_ref[0] = total[HALF:].astype(BF16)

    @pl.when(pl.program_id(0) == 0)
    def _():
        step(far_ref)

    @pl.when(pl.program_id(0) == 1)
    def _():
        step(own_ref)


def side_kernel(order, *refs):
    pieces = refs[:4]
    basis_ref, up_ref, down_ref = refs[4:]
    total = None
    for number in range(4):
        first = pl.multiple_of(order[number] * STEP, 128)
        term = lax.dot_general(
            pieces[number][...],
            basis_ref[:, pl.ds(first, SUB)],
            (((1,), (1,)), ((), ())),
            preferred_element_type=F32,
        )
        total = term if total is None else total + term
    up_ref[...] = total[:HALF].astype(BF16)
    down_ref[...] = total[HALF:].astype(BF16)


def side_product(order, pieces, basis):
    result = jax.ShapeDtypeStruct((HALF, OUT), BF16)
    half = pl.BlockSpec((HALF, COLS), lambda n, order: (0, n))
    return pl.pallas_call(
        side_kernel,
        out_shape=(result, result),
        grid_spec=pltpu.PrefetchScalarGridSpec(
            num_scalar_prefetch=1,
            grid=(pl.cdiv(OUT, COLS),),
            in_specs=[pl.BlockSpec((2 * HALF, SUB), lambda n, order: (0, 0))] * 4
            + [pl.BlockSpec((COLS, FREQ), lambda n, order: (n, 0))],
            out_specs=[half, half],
        ),
        compiler_params=pltpu.CompilerParams(vmem_limit_bytes=60 * MIB),
        cost_estimate=pl.CostEstimate(
            flops=336 * 2688 * 2688, bytes_accessed=10 * MIB, transcendentals=0
        ),
    )(order, *pieces, basis)


def product(order, pieces, own, far):
    result = jax.ShapeDtypeStruct((2, HALF, OUT), BF16)
    half = pl.BlockSpec((1, HALF, COLS), lambda s, n, order: (s, 0, n))
    steps = pl.cdiv(OUT, COLS)
    return pl.pallas_call(
        product_kernel,
        out_shape=(result, result),
        grid_spec=pltpu.PrefetchScalarGridSpec(
            num_scalar_prefetch=1,
            grid=(2, steps),
            in_specs=[pl.BlockSpec((2 * HALF, SUB), lambda s, n, order: (0, 0))] * 4
            + [
                pl.BlockSpec((COLS, FREQ), lambda s, n, order: (jnp.where(s == 1, n, 0), 0)),
                pl.BlockSpec((COLS, FREQ), lambda s, n, order: (jnp.where(s == 0, n, steps - 1), 0)),
            ],
            out_specs=[half, half],
        ),
        compiler_params=pltpu.CompilerParams(vmem_limit_bytes=60 * MIB),
        cost_estimate=pl.CostEstimate(
            flops=2 * 336 * 2688 * 2688, bytes_accessed=18 * MIB, transcendentals=0
        ),
    )(order, *pieces, own, far)


def shards(activations, out_grads, act_basis, grad_basis, eigenvalues, query_ids):
    z, x, k = (lax.axis_index(a) for a in ("z", "x", "k"))

    *eig_parts, eig_sums = cut_eigenvalues(eigenvalues)
    eig = [lax.select_n((x + by) % 4, *eig_parts) for by in range(4)]
    grad_basis_later, *_ = after([grad_basis], *eig)
    eig[1:] = [shift(eig[by], "x", by) for by in (1, 2, 3)]

    window = grad_basis_later[0::2]
    window = jnp.where(k == 0, window, jnp.concatenate([window[HALF:], window[:HALF]], axis=0))
    window = jnp.stack([window[:HALF], shift(window[HALF:], "k", 1)])
    window = jnp.stack([window, shift(window, "h", 1)])
    windows = lax.all_gather(window, ("z", "x"), axis=0).reshape(4, 4, 2, 2, HALF, EBLK)

    tail = jnp.zeros((8, 96), BF16).at[0, :3].set(three(jnp.sum(eig_sums)))
    grad_in = jnp.concatenate([out_grads.astype(BF16), tail], axis=1)
    act_all = gather(activations.astype(BF16), ROW).reshape(TOKENS, OUT)
    grad_all = gather(after(grad_in, act_all), COL).reshape(TOKENS, 768)
    eig_col = jnp.sum(grad_all[0::8, 672:675].astype(F32))

    grad_part = jnp.dot(grad_all[:, :672], grad_basis, preferred_element_type=F32)

    def with_sum(part, total):
        return jnp.concatenate([part.astype(BF16), jnp.zeros((TOKENS, 48), BF16).at[0, :3].set(three(total))], axis=1)

    act_all, eig = lax.optimization_barrier((act_all, eig))
    act_part = jnp.dot(act_all, act_basis, preferred_element_type=F32)
    act_part = (act_part + shift(act_part.astype(BF16), "k", 1).astype(F32)).astype(BF16)
    grad_part = after(grad_part, act_part)
    pair = shift(with_sum(grad_part, eig_col), "h", 1).astype(F32)
    grad_part = grad_part + pair[:, :EBLK]
    pieces = around(with_sum(grad_part, eig_col + jnp.sum(pair[0, EBLK : EBLK + 3])), "z")
    summed = sum(piece.astype(F32) for piece in pieces)
    grad_own = summed[:, :EBLK].astype(BF16)
    damping = 0.1 * jnp.sum(summed[0, EBLK : EBLK + 3]) / (WIDTH * INNER)
    act_cuts = [act_part[:, c * STEP : c * STEP + SUB] for c in range(4)]
    act_sum = lax.select_n(x, *act_cuts).astype(F32)
    for by in (1, 2, 3):
        act_sum += shift(lax.select_n((x + by) % 4, *act_cuts), "x", by).astype(F32)
    grad_rot = jnp.stack(around(after(grad_own, act_sum), "x"))
    place = lax.broadcasted_iota(jnp.int32, (1, SUB), 1) - (SUBOWN - STEP) * x
    act_sum = jnp.where((place >= 0) & (place < SUBOWN), act_sum, 0.0)
    act_rot = (act_sum + shift(act_sum.astype(BF16), "l", 1).astype(F32)).astype(BF16)
    basis_far = shift(act_basis, "k", 1)

    shifted = jnp.stack(eig).astype(F32) + damping

    queries = jnp.arange(NQ, dtype=jnp.int32)
    owned = query_ids[None, :] == queries[:, None]
    masked = jnp.where(owned[:, None, :, None], grad_rot[None], jnp.zeros_like(grad_rot)[None])
    tiles = jnp.einsum("qxtc,tf->qxcf", masked, act_rot, preferred_element_type=F32)
    local_self = jnp.sum(tiles * tiles / shifted[None], axis=(1, 2, 3))
    spread = jnp.zeros((1, 128), F32).at[0, :NQ].set(local_self)
    self_infl = jnp.sum(gather(spread, ALL), axis=0)[0, :NQ] / (WIDTH * INNER)
    scales = 1.0 / jnp.sqrt(self_infl + 1e-06)
    token_scale = jnp.sum(jnp.where(owned, scales[:, None], 0.0), axis=0)
    scaled = grad_rot.astype(F32) * token_scale[None, :, None]
    scaled_high = scaled.astype(BF16)
    scaled_low = (scaled - scaled_high.astype(F32)).astype(BF16)
    both = jnp.concatenate([scaled_high, scaled_low], axis=1)
    act_both = jnp.concatenate([act_rot, act_rot], axis=0)
    total = jnp.einsum("xtc,tf->xcf", both, act_both, preferred_element_type=F32)
    rotated = (total / shifted).astype(BF16)
    rotated, basis_far = lax.optimization_barrier((rotated, basis_far))
    rotated_pair = shift(rotated, "k", 1)

    order = (x - jnp.arange(4, dtype=jnp.int32)) % 4
    lefts = []
    for j in range(4):
        rows = jnp.stack([(z + 3 - j) % 4, (z + 1 + j) % 4]).astype(jnp.int32)
        lefts.append(left_part(rows, order, windows, rotated, rotated_pair))
    summed = [(part.astype(F32) + shift(part, "l", 1).astype(F32)).astype(BF16) for part in lefts]
    ring = None
    sums = []
    for j in range(4):
        pieces = around(summed[j].reshape(2 * HALF, SUB), "x")
        pieces = after(pieces, *(sums[j - 1] if j > 0 else lefts))
        if j == 3:
            break
        up, down = product(order, pieces, act_basis, basis_far)
        if ring is not None:
            up = (up.astype(F32) + ring[0].astype(F32)).astype(BF16)
            down = (down.astype(F32) + ring[1].astype(F32)).astype(BF16)
        sums.append((up, down))
        if j < 2:
            ring = (shift(up, "z", 1), shift(down, "z", 3))

    arrived = [
        lax.optimization_barrier((shift(sums[2][0][side], "z", 1), shift(sums[2][1][side], "z", 3)))
        for side in range(2)
    ]
    done = []
    give = ()
    for side, basis in enumerate((basis_far, act_basis)):
        up, down = side_product(order, after(pieces, *give), basis)
        give = ((down.astype(F32) + arrived[side][1].astype(F32)).astype(BF16),)
        keep = up.astype(F32) + arrived[side][0].astype(F32)
        done.append((keep + shift(give[0], "h", 1).astype(F32)).astype(BF16))
    back = shift(done[0], "k", 1)
    low = jnp.where(k == 0, done[1], back)
    high = jnp.where(k == 0, back, done[1])
    return jnp.concatenate([low, high], axis=0).astype(F32)


def solution(mesh):
    fine = Mesh(mesh.devices.reshape(tuple(SIZES.values())), tuple(SIZES))
    return jax.shard_map(
        shards,
        mesh=fine,
        in_specs=(P(ROW, COL), P(COL, ROW), P(COL, ROW), P(ROW, COL), P(COL, ROW), P()),
        out_specs=P(ROW, COL),
        check_vma=False,
    )
```

```python
import jax
import jax.numpy as jnp
from jax import lax
from jax.experimental import pallas as pl
from jax.experimental.pallas import tpu as pltpu
from jax.sharding import Mesh, PartitionSpec as P

WIDTH = 5376
INNER = 21504
NQ = 8
TOKENS = 128
SIZES = {"z": 4, "h": 2, "x": 4, "l": 2, "k": 2}
ROW = ("z", "h")
COL = ("x", "l", "k")
ALL = ("z", "h", "x", "l", "k")
HALF = 168
FREQ = 2688
SUBOWN = 672
STEP, SUB = 640, 768
COLS = 768
EBLK = 336
OUT = 1344
F32 = jnp.float32
BF16 = jnp.bfloat16
MIB = 1024 * 1024


def shift(array, axis, by):
    size = SIZES[axis]
    return lax.ppermute(array, axis, [(i, (i + by) % size) for i in range(size)])


def around(array, axis):
    return [array] + [shift(array, axis, by) for by in (1, 2, 3)]


def gather(array, axes):
    count = 1
    for axis in axes:
        count *= SIZES[axis]
    spread = jnp.broadcast_to(array[None], (count,) + array.shape)
    return lax.all_to_all(spread, axes, 0, 0, tiled=True)


def after(array, *others):
    return lax.optimization_barrier((array, others))[0]


def cut_kernel(eig_ref, *refs):
    values = eig_ref[...]
    for part in range(4):
        refs[part][...] = values[:, part * STEP : part * STEP + SUB].astype(BF16)
    refs[4][0] = jnp.sum(values.reshape(14, 8, FREQ), axis=0)


def cut_eigenvalues(eigenvalues):
    return pl.pallas_call(
        cut_kernel,
        out_shape=[jax.ShapeDtypeStruct((EBLK, SUB), BF16)] * 4 + [jax.ShapeDtypeStruct((3, 8, FREQ), F32)],
        grid=(3,),
        in_specs=[pl.BlockSpec((112, FREQ), lambda i: (i, 0))],
        out_specs=[pl.BlockSpec((112, SUB), lambda i: (i, 0))] * 4
        + [pl.BlockSpec((1, 8, FREQ), lambda i: (i, 0, 0))],
        compiler_params=pltpu.CompilerParams(vmem_limit_bytes=48 * MIB),
        cost_estimate=pl.CostEstimate(flops=10**6, bytes_accessed=6 * MIB, transcendentals=0),
    )(eigenvalues)


def left_kernel(rows, order, w_ref, own_ref, pair_ref, out_ref):
    total = None
    for part in range(4):
        for side, rot_ref in enumerate((own_ref, pair_ref)):
            term = jnp.dot(w_ref[0, order[part], 0, side], rot_ref[part], preferred_element_type=F32)
            total = term if total is None else total + term
    out_ref[0] = total.astype(BF16)


def left_part(rows, order, windows, own, pair):
    return pl.pallas_call(
        left_kernel,
        out_shape=jax.ShapeDtypeStruct((2, HALF, SUB), BF16),
        grid_spec=pltpu.PrefetchScalarGridSpec(
            num_scalar_prefetch=2,
            grid=(2,),
            in_specs=[pl.BlockSpec((1, 4, 1, 2, HALF, EBLK), lambda i, rows, order: (rows[i], 0, i, 0, 0, 0))]
            + [pl.BlockSpec((4, EBLK, SUB), lambda i, rows, order: (0, 0, 0))] * 2,
            out_specs=pl.BlockSpec((1, HALF, SUB), lambda i, rows, order: (i, 0, 0)),
        ),
        compiler_params=pltpu.CompilerParams(vmem_limit_bytes=54 * MIB),
        cost_estimate=pl.CostEstimate(
            flops=2 * 672 * 1344 * 672, bytes_accessed=6 * MIB, transcendentals=0
        ),
    )(rows, order, windows, own, pair)


def three(value):
    high = value.astype(BF16)
    rest = value - high.astype(F32)
    middle = rest.astype(BF16)
    return jnp.stack([high, middle, (rest - middle.astype(F32)).astype(BF16)])


def half_kernel(rows, order, w_ref, rot_ref, *refs):
    total = refs[0][0] if len(refs) == 2 else None
    for part in range(4):
        term = jnp.dot(w_ref[0, order[part], 0, 0], rot_ref[part], preferred_element_type=F32)
        total = term if total is None else total + term
    refs[-1][0] = total.astype(refs[-1].dtype)


def left_half(rows, order, windows, rotated, side, begun):
    block = pl.BlockSpec((1, HALF, SUB), lambda i, rows, order: (i, 0, 0))
    return pl.pallas_call(
        half_kernel,
        out_shape=jax.ShapeDtypeStruct((2, HALF, SUB), BF16 if begun else F32),
        grid_spec=pltpu.PrefetchScalarGridSpec(
            num_scalar_prefetch=2,
            grid=(2,),
            in_specs=[
                pl.BlockSpec((1, 4, 1, 1, HALF, EBLK), lambda i, rows, order: (rows[i], 0, i, side, 0, 0)),
                pl.BlockSpec((4, EBLK, SUB), lambda i, rows, order: (0, 0, 0)),
            ]
            + [block] * len(begun),
            out_specs=block,
        ),
        compiler_params=pltpu.CompilerParams(vmem_limit_bytes=54 * MIB),
        cost_estimate=pl.CostEstimate(
            flops=672 * 1344 * 672, bytes_accessed=3 * MIB, transcendentals=0
        ),
    )(rows, order, windows, rotated, *begun)


def product_kernel(order, *refs):
    pieces = refs[:4]
    own_ref, far_ref, up_ref, down_ref = refs[4:]

    def step(basis_ref):
        total = None
        for number in range(4):
            first = pl.multiple_of(order[number] * STEP, 128)
            term = lax.dot_general(
                pieces[number][...],
                basis_ref[:, pl.ds(first, SUB)],
                (((1,), (1,)), ((), ())),
                preferred_element_type=F32,
            )
            total = term if total is None else total + term
        up_ref[0] = total[:HALF].astype(BF16)
        down_ref[0] = total[HALF:].astype(BF16)

    @pl.when(pl.program_id(0) == 0)
    def _():
        step(far_ref)

    @pl.when(pl.program_id(0) == 1)
    def _():
        step(own_ref)


def side_kernel(order, *refs):
    pieces = refs[:4]
    basis_ref, up_ref, down_ref = refs[4:]
    total = None
    for number in range(4):
        first = pl.multiple_of(order[number] * STEP, 128)
        term = lax.dot_general(
            pieces[number][...],
            basis_ref[:, pl.ds(first, SUB)],
            (((1,), (1,)), ((), ())),
            preferred_element_type=F32,
        )
        total = term if total is None else total + term
    up_ref[...] = total[:HALF].astype(BF16)
    down_ref[...] = total[HALF:].astype(BF16)


def side_product(order, pieces, basis):
    result = jax.ShapeDtypeStruct((HALF, OUT), BF16)
    half = pl.BlockSpec((HALF, COLS), lambda n, order: (0, n))
    return pl.pallas_call(
        side_kernel,
        out_shape=(result, result),
        grid_spec=pltpu.PrefetchScalarGridSpec(
            num_scalar_prefetch=1,
            grid=(pl.cdiv(OUT, COLS),),
            in_specs=[pl.BlockSpec((2 * HALF, SUB), lambda n, order: (0, 0))] * 4
            + [pl.BlockSpec((COLS, FREQ), lambda n, order: (n, 0))],
            out_specs=[half, half],
        ),
        compiler_params=pltpu.CompilerParams(vmem_limit_bytes=60 * MIB),
        cost_estimate=pl.CostEstimate(
            flops=336 * 2688 * 2688, bytes_accessed=10 * MIB, transcendentals=0
        ),
    )(order, *pieces, basis)


def product(order, pieces, own, far):
    result = jax.ShapeDtypeStruct((2, HALF, OUT), BF16)
    half = pl.BlockSpec((1, HALF, COLS), lambda s, n, order: (s, 0, n))
    steps = pl.cdiv(OUT, COLS)
    return pl.pallas_call(
        product_kernel,
        out_shape=(result, result),
        grid_spec=pltpu.PrefetchScalarGridSpec(
            num_scalar_prefetch=1,
            grid=(2, steps),
            in_specs=[pl.BlockSpec((2 * HALF, SUB), lambda s, n, order: (0, 0))] * 4
            + [
                pl.BlockSpec((COLS, FREQ), lambda s, n, order: (jnp.where(s == 1, n, 0), 0)),
                pl.BlockSpec((COLS, FREQ), lambda s, n, order: (jnp.where(s == 0, n, steps - 1), 0)),
            ],
            out_specs=[half, half],
        ),
        compiler_params=pltpu.CompilerParams(vmem_limit_bytes=60 * MIB),
        cost_estimate=pl.CostEstimate(
            flops=2 * 336 * 2688 * 2688, bytes_accessed=18 * MIB, transcendentals=0
        ),
    )(order, *pieces, own, far)


def shards(activations, out_grads, act_basis, grad_basis, eigenvalues, query_ids):
    z, x, k = (lax.axis_index(a) for a in ("z", "x", "k"))

    *eig_parts, eig_sums = cut_eigenvalues(eigenvalues)
    eig = [lax.select_n((x + by) % 4, *eig_parts) for by in range(4)]
    grad_basis_later, *_ = after([grad_basis], *eig)
    eig[1:] = [shift(eig[by], "x", by) for by in (1, 2, 3)]

    window = grad_basis_later[0::2]
    window = jnp.where(k == 0, window, jnp.concatenate([window[HALF:], window[:HALF]], axis=0))
    window = jnp.stack([window[:HALF], shift(window[HALF:], "k", 1)])
    window = jnp.stack([window, shift(window, "h", 1)])
    windows = lax.all_gather(window, ("z", "x"), axis=0).reshape(4, 4, 2, 2, HALF, EBLK)

    tail = jnp.zeros((8, 96), BF16).at[0, :3].set(three(jnp.sum(eig_sums)))
    grad_in = jnp.concatenate([out_grads.astype(BF16), tail], axis=1)
    act_all = gather(activations.astype(BF16), ROW).reshape(TOKENS, OUT)
    grad_all = gather(after(grad_in, act_all), COL).reshape(TOKENS, 768)
    eig_col = jnp.sum(grad_all[0::8, 672:675].astype(F32))

    grad_part = jnp.dot(grad_all[:, :672], grad_basis, preferred_element_type=F32)

    def with_sum(part, total):
        return jnp.concatenate([part.astype(BF16), jnp.zeros((TOKENS, 48), BF16).at[0, :3].set(three(total))], axis=1)

    act_all, eig = lax.optimization_barrier((act_all, eig))
    act_part = jnp.dot(act_all, act_basis, preferred_element_type=F32)
    act_part = (act_part + shift(act_part.astype(BF16), "k", 1).astype(F32)).astype(BF16)
    grad_part = after(grad_part, act_part)
    pair = shift(with_sum(grad_part, eig_col), "h", 1).astype(F32)
    grad_part = grad_part + pair[:, :EBLK]
    pieces = around(with_sum(grad_part, eig_col + jnp.sum(pair[0, EBLK : EBLK + 3])), "z")
    summed = sum(piece.astype(F32) for piece in pieces)
    grad_own = summed[:, :EBLK].astype(BF16)
    damping = 0.1 * jnp.sum(summed[0, EBLK : EBLK + 3]) / (WIDTH * INNER)
    act_cuts = [act_part[:, c * STEP : c * STEP + SUB] for c in range(4)]
    act_sum = lax.select_n(x, *act_cuts).astype(F32)
    for by in (1, 2, 3):
        act_sum += shift(lax.select_n((x + by) % 4, *act_cuts), "x", by).astype(F32)
    grad_rot = jnp.stack(around(after(grad_own, act_sum), "x"))
    place = lax.broadcasted_iota(jnp.int32, (1, SUB), 1) - (SUBOWN - STEP) * x
    act_sum = jnp.where((place >= 0) & (place < SUBOWN), act_sum, 0.0)
    act_rot = (act_sum + shift(act_sum.astype(BF16), "l", 1).astype(F32)).astype(BF16)
    basis_far = shift(act_basis, "k", 1)

    shifted = jnp.stack(eig).astype(F32) + damping

    queries = jnp.arange(NQ, dtype=jnp.int32)
    owned = query_ids[None, :] == queries[:, None]
    masked = jnp.where(owned[:, None, :, None], grad_rot[None], jnp.zeros_like(grad_rot)[None])
    tiles = jnp.einsum("qxtc,tf->qxcf", masked, act_rot, preferred_element_type=F32)
    local_self = jnp.sum(tiles * tiles / shifted[None], axis=(1, 2, 3))
    spread = jnp.zeros((1, 128), F32).at[0, :NQ].set(local_self)
    self_infl = jnp.sum(gather(spread, ALL), axis=0)[0, :NQ] / (WIDTH * INNER)
    scales = 1.0 / jnp.sqrt(self_infl + 1e-06)
    token_scale = jnp.sum(jnp.where(owned, scales[:, None], 0.0), axis=0)
    scaled = grad_rot.astype(F32) * token_scale[None, :, None]
    scaled_high = scaled.astype(BF16)
    scaled_low = (scaled - scaled_high.astype(F32)).astype(BF16)
    both = jnp.concatenate([scaled_high, scaled_low], axis=1)
    act_both = jnp.concatenate([act_rot, act_rot], axis=0)
    total = jnp.einsum("xtc,tf->xcf", both, act_both, preferred_element_type=F32)
    rotated = (total / shifted).astype(BF16)
    rotated, basis_far = lax.optimization_barrier((rotated, basis_far))
    rotated_pair = shift(rotated, "k", 1)

    order = (x - jnp.arange(4, dtype=jnp.int32)) % 4
    lefts = []
    for j in range(4):
        rows = jnp.stack([(z + 3 - j) % 4, (z + 1 + j) % 4]).astype(jnp.int32)
        if j == 0:
            begun = left_half(rows, order, windows, rotated, 0, ())
            lefts.append(left_half(rows, order, windows, rotated_pair, 1, (begun,)))
        else:
            lefts.append(left_part(rows, order, windows, rotated, rotated_pair))
    summed = [(part.astype(F32) + shift(part, "l", 1).astype(F32)).astype(BF16) for part in lefts]
    ring = None
    sums = []
    for j in range(4):
        pieces = around(summed[j].reshape(2 * HALF, SUB), "x")
        pieces = after(pieces, *(sums[j - 1] if j > 0 else lefts))
        if j == 3:
            break
        up, down = product(order, pieces, act_basis, basis_far)
        if ring is not None:
            up = (up.astype(F32) + ring[0].astype(F32)).astype(BF16)
            down = (down.astype(F32) + ring[1].astype(F32)).astype(BF16)
        sums.append((up, down))
        if j < 2:
            ring = (shift(up, "z", 1), shift(down, "z", 3))

    arrived = [
        lax.optimization_barrier((shift(sums[2][0][side], "z", 1), shift(sums[2][1][side], "z", 3)))
        for side in range(2)
    ]
    done = []
    give = ()
    for side, basis in enumerate((basis_far, act_basis)):
        up, down = side_product(order, after(pieces, *give), basis)
        give = ((down.astype(F32) + arrived[side][1].astype(F32)).astype(BF16),)
        keep = up.astype(F32) + arrived[side][0].astype(F32)
        done.append((keep + shift(give[0], "h", 1).astype(F32)).astype(BF16))
    back = shift(done[0], "k", 1)
    low = jnp.where(k == 0, done[1], back)
    high = jnp.where(k == 0, back, done[1])
    return jnp.concatenate([low, high], axis=0).astype(F32)


def solution(mesh):
    fine = Mesh(mesh.devices.reshape(tuple(SIZES.values())), tuple(SIZES))
    return jax.shard_map(
        shards,
        mesh=fine,
        in_specs=(P(ROW, COL), P(COL, ROW), P(COL, ROW), P(ROW, COL), P(COL, ROW), P()),
        out_specs=P(ROW, COL),
        check_vma=False,
    )
```
